1024 devices in a mesh: energy: 256 (over z, y, x_lo), slab: 4 (over x_hi, core).
Axes of the slice: x: 4 (x_hi: 2, x_lo: 2; x = x_hi * 2 + x_lo), y: 4, z: 32, core: 2. Of those that a mesh axis runs over, the one named last changes fastest.
Arguments:
- green_free: bfloat16 [256, 4, 2, 256, 256], P('energy', 'slab')
- coupling: bfloat16 [4, 2, 256, 256], P('slab'), may hold values from -0.25 to 0.25
- screened: bfloat16 [8, 4, 2, 256, 256], P(None, 'slab'), may hold values from -6 to 6
- shift_offsets: int32 [8], replicated, may hold values from -1 to 1, as said below
Outputs:
- green: bfloat16 [256, 4, 2, 256, 256], P('energy', 'slab')
- sigma: float32 [256, 4, 2, 256, 256], P('energy', 'slab')
The draws below stay inside these ranges and needn't reach their ends.
Inputs may be any that keep to these rules, and one draw needn't show every extreme that they name: `shift_offsets`: offsets lie within one device's energy points on either side; both ends, -1 and 1, occur in every draw.
All inputs are finite; a program needn't handle non-finite values.
Results may differ from the reference program's by a relative error of at most 0.0061.
Values may be sent and summed in bfloat16 or wider, within the bound.
A program may use at most 32 MiB of HBM per device.

```python
import math
import jax
import jax.numpy as jnp
from jax import lax

ORB = 256
E_DEV = 1
SHIFTS = 8
NE = 256
NS = 4


def draw_green_free(key, part):
    first_key = jax.random.fold_in(key, 0)
    third_key = jax.random.fold_in(key, 2)
    shape = (NE, NS, 2, ORB, ORB)
    noise = jax.random.normal(first_key, shape, jnp.float32)
    diagonal = jax.random.uniform(third_key, (NE, NS, ORB), jnp.float32, 0.7, 1.3)
    noise = noise * (0.25 / math.sqrt(ORB))
    identity = jnp.eye(ORB, dtype=jnp.float32)
    real = noise[:, :, 0] + diagonal[..., None] * identity
    whole = jnp.stack([real, noise[:, :, 1]], axis=2)
    return whole.astype(jnp.bfloat16)


def draw_shift_offsets(key, part):
    value_key = jax.random.fold_in(key, 11)
    place_key = jax.random.fold_in(key, 23)
    values = jax.random.randint(value_key, (SHIFTS,), -E_DEV, E_DEV + 1, dtype=jnp.int32)
    places = jax.random.permutation(place_key, SHIFTS)
    values = values.at[places[0]].set(E_DEV).at[places[1]].set(-E_DEV)
    return values.astype(jnp.int32)


def block_scale(stream_key, extent, cuts, smallest, largest):
    level, own = 1.0, jax.random.fold_in(stream_key, 6)
    for axis_at, blocks in cuts:
        steps = jnp.exp(jax.random.uniform(jax.random.fold_in(own, axis_at), (blocks,), jnp.float32, smallest / len(cuts), largest / len(cuts)))
        level = level * jnp.repeat(steps, extent[axis_at] // blocks).reshape([-1 if axis == axis_at else 1 for axis in range(len(extent))])
    return level


def gaussian(key, shape, deviation, limit, cuts=(), kind=jnp.bfloat16):
    factor_of = block_scale(key, shape, cuts, -0.22, 0.18) if cuts else 1.0
    drawn = jax.random.normal(key, shape, jnp.float32) * deviation * factor_of
    return jnp.minimum(jnp.maximum(drawn, -limit), limit).astype(kind)


def setup_inputs(seed: int = 0) -> dict:
    key_list = jax.random.split(jax.random.key(seed), 5)
    green_free = draw_green_free(jax.random.fold_in(key_list[4], 71), 0)
    coupling = gaussian(key_list[1], (NS, 2, ORB, ORB), (5 * ORB // 2) ** -0.5, 0.25, ((0, 4),))
    screened = gaussian(key_list[2], (SHIFTS, NS, 2, ORB, ORB), 1.0, 6.0, ((1, 4),))
    shift_offsets = draw_shift_offsets(jax.random.fold_in(key_list[4], 71), 0)
    return dict(green_free=green_free, coupling=coupling, screened=screened, shift_offsets=shift_offsets)


def complex_product(first, second, form):
    first_re = first[..., 0, :, :].astype(jnp.float32)
    first_im = first[..., 1, :, :].astype(jnp.float32)
    second_re = second[..., 0, :, :].astype(jnp.float32)
    second_im = second[..., 1, :, :].astype(jnp.float32)
    real = jnp.einsum(form, first_re, second_re) - jnp.einsum(form, first_im, second_im)
    imag = jnp.einsum(form, first_re, second_im) + jnp.einsum(form, first_im, second_re)
    return jnp.stack([real, imag], axis=-3)


def adjoint(block):
    real = jnp.swapaxes(block[..., 0, :, :], -1, -2)
    imag = -jnp.swapaxes(block[..., 1, :, :], -1, -2)
    return jnp.stack([real, imag], axis=-3)


def reference(green_free, coupling, screened, shift_offsets):
    left_map = complex_product(green_free, coupling, "esij,sjk->esik").astype(jnp.bfloat16)
    right_map = complex_product(adjoint(coupling), green_free, "sij,esjk->esik").astype(jnp.bfloat16)

    def advance(carry, slab_data):
        left_slab, right_slab, free_slab = slab_data
        middle = complex_product(left_slab, carry, "eij,ejk->eik").astype(jnp.bfloat16)
        fresh = (free_slab.astype(jnp.float32) + complex_product(middle, right_slab, "eij,ejk->eik")).astype(jnp.bfloat16)
        return fresh, fresh

    start = jnp.zeros((green_free.shape[0],) + green_free.shape[2:], jnp.bfloat16)
    _, swept = lax.scan(advance, start, (jnp.moveaxis(left_map, 1, 0), jnp.moveaxis(right_map, 1, 0), jnp.moveaxis(green_free, 1, 0)))
    green = jnp.moveaxis(swept, 0, 1)
    real_sum = jnp.zeros(green.shape[:2] + green.shape[3:], jnp.float32)
    imag_sum = jnp.zeros(green.shape[:2] + green.shape[3:], jnp.float32)
    for shift_no in range(SHIFTS):
        moved = jnp.roll(green, shift_offsets[shift_no], axis=0).astype(jnp.float32)
        weight = screened[shift_no].astype(jnp.float32)
        moved_re = moved[:, :, 0]
        moved_im = moved[:, :, 1]
        weight_re = weight[None, :, 0]
        weight_im = weight[None, :, 1]
        real_sum = real_sum + moved_re * weight_re - moved_im * weight_im
        imag_sum = imag_sum + moved_re * weight_im + moved_im * weight_re
    sigma = jnp.stack([-imag_sum, real_sum], axis=2)
    return green, sigma
```

```python
import functools

import jax
import jax.numpy as jnp
from jax import lax
from jax.experimental import pallas as pl
from jax.experimental.pallas import tpu as pltpu
from jax.sharding import PartitionSpec as P

MESH = pl.DeviceIdType.MESH
CHUNKS = 4


def dot(a, b):
    return jnp.dot(a, b, preferred_element_type=jnp.float32)


def dot_t(a, b):
    return lax.dot_general(a, b, (((0,), (0,)), ((), ())), preferred_element_type=jnp.float32)


def complex_dot(first, second_re, second_im):
    half = first.shape[0] // 2
    by_re = dot(first, second_re)
    by_im = dot(first, second_im)
    return by_re[:half] - by_im[half:], by_im[:half] + by_re[half:]


def kernel(
    energies,
    slabs,
    shift_ref,
    free_hbm,
    coup_hbm,
    scr_hbm,
    green,
    sig,
    free,
    coup,
    scr,
    left,
    right,
    prev,
    near,
    far,
    weight,
    load_sem,
    chain_send,
    chain_recv,
    near_send,
    near_recv,
    far_send,
    far_recv,
):
    e = lax.axis_index("energy")
    s = lax.axis_index("slab")
    shifts = scr.shape[0]
    orb = free.shape[1]
    rows = orb // CHUNKS
    parity = lax.rem(e, 2)
    partner = e + 1 - 2 * parity
    onward = lax.rem(e + 2 - 4 * parity + energies, energies)
    behind = lax.rem(e - 2 + 4 * parity + energies, energies)

    load_free = pltpu.make_async_copy(free_hbm.at[0, 0], free, load_sem.at[0])
    load_coup = pltpu.make_async_copy(coup_hbm.at[0], coup, load_sem.at[1])
    load_free.start()
    load_coup.start()
    loads = []
    for k in range(shifts):
        load = pltpu.make_async_copy(scr_hbm.at[k, 0], scr.at[k], load_sem.at[2 + k])
        load.start()
        loads.append(load)

    barrier = pltpu.get_barrier_semaphore()
    pl.semaphore_signal(barrier, inc=1, device_id=(partner, s), device_id_type=MESH)
    pl.semaphore_signal(barrier, inc=1, device_id=(behind, s), device_id_type=MESH)

    @pl.when(s > 0)
    def _():
        pl.semaphore_signal(barrier, inc=1, device_id=(e, s - 1), device_id_type=MESH)

    chain = pltpu.make_async_remote_copy(
        src_ref=green,
        dst_ref=prev,
        send_sem=chain_send,
        recv_sem=chain_recv,
        device_id=(e, lax.rem(s + 1, slabs)),
        device_id_type=MESH,
    )

    def to_partner(c):
        part = pl.ds(c * rows, rows)
        return pltpu.make_async_remote_copy(
            src_ref=green.at[:, part],
            dst_ref=near.at[:, part],
            send_sem=near_send.at[c],
            recv_sem=near_recv.at[c],
            device_id=(partner, s),
            device_id_type=MESH,
        )

    def to_onward(c):
        part = pl.ds(c * rows, rows)
        return pltpu.make_async_remote_copy(
            src_ref=near.at[:, part],
            dst_ref=far.at[:, part],
            send_sem=far_send.at[c],
            recv_sem=far_recv.at[c],
            device_id=(onward, s),
            device_id_type=MESH,
        )

    def sum_weights():
        for load in loads:
            load.wait()
        near_shift = 2 * parity - 1

        @pl.loop(0, orb // 16)
        def _(step):
            part = pl.ds(pl.multiple_of(step * 16, 16), 16)
            at = [jnp.zeros((2, 16, orb), jnp.float32) for _ in range(3)]
            for k in range(shifts):
                block = scr[k, :, part, :].astype(jnp.float32)
                for slot, value in enumerate((0, near_shift, -near_shift)):
                    at[slot] = at[slot] + jnp.where(shift_ref[k] == value, block, 0.0)
            for slot in range(3):
                weight[slot, :, part, :] = at[slot]

    load_free.wait()

    @pl.when(s == 0)
    def _():
        green[...] = free[...]
        load_coup.wait()

    @pl.when(s > 0)
    def _():
        load_coup.wait()
        stacked = free[...].reshape(2 * orb, orb)
        re, im = complex_dot(stacked, coup[0], coup[1])
        left[0] = re.astype(jnp.bfloat16)
        left[1] = im.astype(jnp.bfloat16)
        rr = dot_t(coup[0], free[0]) + dot_t(coup[1], free[1])
        ri = dot_t(coup[0], free[1]) - dot_t(coup[1], free[0])
        right[0] = rr.astype(jnp.bfloat16)
        right[1] = ri.astype(jnp.bfloat16)

    @pl.when(s >= 2)
    def _():
        sum_weights()

    @pl.when(s < slabs - 1)
    def _():
        pl.semaphore_wait(barrier, 3)

    @pl.when(s == slabs - 1)
    def _():
        pl.semaphore_wait(barrier, 2)

    @pl.when(s > 0)
    def _():
        chain.wait_recv()
        re, im = complex_dot(left[...].reshape(2 * orb, orb), prev[0], prev[1])
        middle = jnp.concatenate([re.astype(jnp.bfloat16), im.astype(jnp.bfloat16)], axis=0)
        re, im = complex_dot(middle, right[0], right[1])
        green[0] = (free[0].astype(jnp.float32) + re).astype(jnp.bfloat16)
        green[1] = (free[1].astype(jnp.float32) + im).astype(jnp.bfloat16)

    @pl.when(s < slabs - 1)
    def _():
        chain.start()

    for c in range(CHUNKS):
        to_partner(c).start()

    @pl.when(s < 2)
    def _():
        sum_weights()

    def term(block, slot, part):
        re = block[0, part, :].astype(jnp.float32)
        im = block[1, part, :].astype(jnp.float32)
        wr = weight[slot, 0, part, :]
        wi = weight[slot, 1, part, :]
        return re * wr - im * wi, re * wi + im * wr

    for c in range(CHUNKS):
        part = pl.ds(c * rows, rows)
        to_partner(c).wait_recv()
        to_onward(c).start()
        own = term(green, 0, part)
        beside = term(near, 1, part)
        sig[0, part, :] = -(own[1] + beside[1])
        sig[1, part, :] = own[0] + beside[0]

    for c in range(CHUNKS):
        part = pl.ds(c * rows, rows)
        to_onward(c).wait_recv()
        beyond = term(far, 2, part)
        sig[0, part, :] = sig[0, part, :] - beyond[1]
        sig[1, part, :] = sig[1, part, :] + beyond[0]

    @pl.when(s < slabs - 1)
    def _():
        chain.wait_send()

    for c in range(CHUNKS):
        to_partner(c).wait_send()
        to_onward(c).wait_send()


def shards(energies, slabs, green_free, coupling, screened, shift_offsets):
    orb = green_free.shape[-1]
    shifts = screened.shape[0]
    block = (2, orb, orb)
    hbm = pl.BlockSpec(memory_space=pltpu.HBM)
    vmem = pl.BlockSpec(memory_space=pltpu.VMEM)
    dma = pltpu.SemaphoreType.DMA
    green, sigma = pl.pallas_call(
        functools.partial(kernel, energies, slabs),
        out_shape=(
            jax.ShapeDtypeStruct(block, jnp.bfloat16),
            jax.ShapeDtypeStruct(block, jnp.float32),
        ),
        in_specs=[pl.BlockSpec(memory_space=pltpu.SMEM), hbm, hbm, hbm],
        out_specs=(vmem, vmem),
        scratch_shapes=[
            pltpu.VMEM(block, jnp.bfloat16),
            pltpu.VMEM(block, jnp.bfloat16),
            pltpu.VMEM((shifts, *block), jnp.bfloat16),
            pltpu.VMEM(block, jnp.bfloat16),
            pltpu.VMEM(block, jnp.bfloat16),
            pltpu.VMEM(block, jnp.bfloat16),
            pltpu.VMEM(block, jnp.bfloat16),
            pltpu.VMEM(block, jnp.bfloat16),
            pltpu.VMEM((3, *block), jnp.float32),
            dma((2 + shifts,)),
            dma,
            dma,
            dma((CHUNKS,)),
            dma((CHUNKS,)),
            dma((CHUNKS,)),
            dma((CHUNKS,)),
        ],
        compiler_params=pltpu.CompilerParams(
            collective_id=0, has_side_effects=True, vmem_limit_bytes=57 * 2**20
        ),
    )(shift_offsets, green_free, coupling, screened)
    return green.reshape(green_free.shape), sigma.reshape(green_free.shape)


def solution(mesh):
    placed = (
        P("energy", "slab", None, None, None),
        P("slab", None, None, None),
        P(None, "slab", None, None, None),
        P(),
    )
    return jax.shard_map(
        functools.partial(shards, mesh.shape["energy"], mesh.shape["slab"]),
        mesh=mesh,
        in_specs=placed,
        out_specs=(P("energy", "slab", None, None, None), P("energy", "slab", None, None, None)),
        check_vma=False,
    )
```

```python
import functools

import jax
import jax.numpy as jnp
from jax import lax
from jax.experimental import pallas as pl
from jax.experimental.pallas import tpu as pltpu
from jax.sharding import PartitionSpec as P

MESH = pl.DeviceIdType.MESH
CHUNKS = 4
STEPS = 2
CHAIN, CROSS, BEYOND, NEAR, FAR, FREE_NEAR, FREE_FAR = range(7)
OWN, BESIDE, REMOTE = range(3)


def dot(a, b):
    return jnp.dot(a, b, preferred_element_type=jnp.float32)


def dot_t(a, b):
    return lax.dot_general(a, b, (((0,), (0,)), ((), ())), preferred_element_type=jnp.float32)


def complex_dot(first, second_re, second_im):
    half = first.shape[0] // 2
    by_re = dot(first, second_re)
    by_im = dot(first, second_im)
    return by_re[:half] - by_im[half:], by_im[:half] + by_re[half:]


def kernel(
    energies,
    shift_ref,
    free_hbm,
    coup_hbm,
    scr_hbm,
    green,
    sig,
    free,
    coup,
    scr,
    left,
    right,
    middle,
    chain_in,
    cross_in,
    beyond_in,
    near,
    far,
    free_near,
    free_far,
    weight,
    load_sem,
    send_sem,
    recv_sem,
):
    e = lax.axis_index("energy")
    s = lax.axis_index("slab")
    shifts = scr.shape[0]
    orb = free.shape[1]
    rows = orb // CHUNKS
    parity = lax.rem(e, 2)
    partner = e + 1 - 2 * parity
    onward = lax.rem(e + 2 - 4 * parity + energies, energies)
    behind = lax.rem(e - 2 + 4 * parity + energies, energies)
    landing = (chain_in, cross_in, beyond_in, near, far, free_near, free_far)

    load_free = pltpu.make_async_copy(free_hbm.at[0, 0], free, load_sem.at[0])
    load_coup = pltpu.make_async_copy(coup_hbm.at[0], coup, load_sem.at[1])
    loads = [
        pltpu.make_async_copy(scr_hbm.at[k, 0], scr.at[k], load_sem.at[2 + k])
        for k in range(shifts)
    ]
    barrier = pltpu.get_barrier_semaphore()

    def greet(device):
        pl.semaphore_signal(barrier, inc=1, device_id=device, device_id_type=MESH)

    greet((partner, s))
    greet((behind, s))

    @pl.when(s == 1)
    def _():
        greet((e, 0))

    @pl.when(s == 2)
    def _():
        greet((partner, 1))

    @pl.when(s == 3)
    def _():
        greet((e, 2))

    load_free.start()
    load_coup.start()
    for load in loads:
        load.start()

    def move(kind, source, device, c):
        part = pl.ds(c * rows, rows)
        return pltpu.make_async_remote_copy(
            src_ref=source.at[:, part],
            dst_ref=landing[kind].at[:, part],
            send_sem=send_sem.at[kind, c],
            recv_sem=recv_sem.at[kind, c],
            device_id=device,
            device_id_type=MESH,
        )

    def arrived(kind, c):
        move(kind, free, (partner, s), c).wait_recv()

    def all_arrived(kind):
        for c in range(CHUNKS):
            arrived(kind, c)

    def sent(kind):
        for c in range(CHUNKS):
            move(kind, free, (partner, s), c).wait_send()

    def maps(block, slot):
        re, im = complex_dot(block[...].reshape(2 * orb, orb), coup[0], coup[1])
        left[slot, 0] = re.astype(jnp.bfloat16)
        left[slot, 1] = im.astype(jnp.bfloat16)
        re = dot_t(coup[0], block[0]) + dot_t(coup[1], block[1])
        im = dot_t(coup[0], block[1]) - dot_t(coup[1], block[0])
        right[slot, 0] = re.astype(jnp.bfloat16)
        right[slot, 1] = im.astype(jnp.bfloat16)

    def advance(slot, before, block, result, done=None):
        re, im = complex_dot(left[slot].reshape(2 * orb, orb), before[0], before[1])
        middle[0] = re.astype(jnp.bfloat16)
        middle[1] = im.astype(jnp.bfloat16)
        high = orb // STEPS
        for step in range(STEPS):
            part = pl.ds(step * high, high)
            stacked = middle[:, part, :].reshape(2 * high, orb)
            re, im = complex_dot(stacked, right[slot, 0], right[slot, 1])
            result[0, part, :] = (block[0, part, :].astype(jnp.float32) + re).astype(jnp.bfloat16)
            result[1, part, :] = (block[1, part, :].astype(jnp.float32) + im).astype(jnp.bfloat16)
            if done is not None:
                for c in range(step * CHUNKS // STEPS, (step + 1) * CHUNKS // STEPS):
                    done(c)

    def sum_weights():
        for load in loads:
            load.wait()
        near_shift = 2 * parity - 1

        @pl.loop(0, orb // 16)
        def _(step):
            part = pl.ds(pl.multiple_of(step * 16, 16), 16)
            total = [jnp.zeros((2, 16, orb), jnp.float32) for _ in range(3)]
            for k in range(shifts):
                block = scr[k, :, part, :].astype(jnp.float32)
                for slot, value in enumerate((0, near_shift, -near_shift)):
                    total[slot] = total[slot] + jnp.where(shift_ref[k] == value, block, 0.0)
            for slot in range(3):
                weight[slot, :, part, :] = total[slot]

    def term(block, slot, part):
        re = block[0, part, :].astype(jnp.float32)
        im = block[1, part, :].astype(jnp.float32)
        weight_re = weight[slot, 0, part, :]
        weight_im = weight[slot, 1, part, :]
        return re * weight_re - im * weight_im, re * weight_im + im * weight_re

    def begin_sigma(c):
        part = pl.ds(c * rows, rows)
        own = term(green, OWN, part)
        beside = term(near, BESIDE, part)
        sig[0, part, :] = -(own[1] + beside[1])
        sig[1, part, :] = own[0] + beside[0]

    def end_sigma(c):
        part = pl.ds(c * rows, rows)
        remote = term(far, REMOTE, part)
        sig[0, part, :] = sig[0, part, :] - remote[1]
        sig[1, part, :] = sig[1, part, :] + remote[0]

    @pl.when(s == 0)
    def _():
        load_free.wait()
        pl.semaphore_wait(barrier, 3)
        for c in range(CHUNKS):
            move(CHAIN, free, (e, 1), c).start()
        for c in range(CHUNKS):
            move(NEAR, free, (partner, s), c).start()
        green[...] = free[...]
        sum_weights()
        for c in range(CHUNKS):
            arrived(NEAR, c)
            move(FAR, near, (onward, s), c).start()
            begin_sigma(c)
        for c in range(CHUNKS):
            arrived(FAR, c)
            end_sigma(c)
        load_coup.wait()
        sent(CHAIN)
        sent(NEAR)
        sent(FAR)

    @pl.when(s == 1)
    def _():
        load_free.wait()
        load_coup.wait()
        maps(free, OWN)
        pl.semaphore_wait(barrier, 3)
        all_arrived(CHAIN)
        advance(OWN, chain_in, free, green, lambda c: move(CROSS, green, (partner, 2), c).start())
        for c in range(CHUNKS):
            move(NEAR, green, (partner, s), c).start()
        sum_weights()
        for c in range(CHUNKS):
            arrived(NEAR, c)
            move(CHAIN, near, (partner, 2), c).start()
            move(FAR, near, (onward, s), c).start()
            begin_sigma(c)
        for c in range(CHUNKS):
            arrived(FAR, c)
            end_sigma(c)
        sent(CROSS)
        sent(NEAR)
        sent(CHAIN)
        sent(FAR)

    @pl.when(s == 2)
    def _():
        load_free.wait()
        pl.semaphore_wait(barrier, 3)
        for c in range(CHUNKS):
            move(FREE_NEAR, free, (partner, s), c).start()
        load_coup.wait()
        maps(free, OWN)
        sum_weights()
        all_arrived(FREE_NEAR)
        maps(free_near, BESIDE)
        all_arrived(CROSS)

        def hand_on(c):
            move(FAR, near, (onward, s), c).start()
            move(CROSS, near, (e, 3), c).start()

        advance(BESIDE, cross_in, free_near, near, hand_on)
        all_arrived(CHAIN)
        advance(OWN, chain_in, free, green, lambda c: move(CHAIN, green, (e, 3), c).start())
        for c in range(CHUNKS):
            arrived(FAR, c)
            move(BEYOND, far, (e, 3), c).start()
            begin_sigma(c)
            end_sigma(c)
        sent(FREE_NEAR)
        sent(FAR)
        sent(CROSS)
        sent(CHAIN)
        sent(BEYOND)

    @pl.when(s == 3)
    def _():
        load_free.wait()
        load_coup.wait()
        maps(free, OWN)
        sum_weights()
        pl.semaphore_wait(barrier, 2)
        for c in range(CHUNKS):
            move(FREE_NEAR, free, (partner, s), c).start()
        for c in range(CHUNKS):
            arrived(FREE_NEAR, c)
            move(FREE_FAR, free_near, (onward, s), c).start()
        maps(free_near, BESIDE)
        all_arrived(CROSS)
        advance(BESIDE, cross_in, free_near, near)
        all_arrived(FREE_FAR)
        maps(free_far, REMOTE)
        all_arrived(CHAIN)
        advance(OWN, chain_in, free, green)
        for c in range(CHUNKS):
            begin_sigma(c)
        all_arrived(BEYOND)
        advance(REMOTE, beyond_in, free_far, far, end_sigma)
        sent(FREE_NEAR)
        sent(FREE_FAR)


def store(green, sig, green_hbm, sigma_hbm, sem):
    copies = [
        pltpu.make_async_copy(green, green_hbm.at[0, 0], sem.at[0]),
        pltpu.make_async_copy(sig.at[0], sigma_hbm.at[0, 0, 0], sem.at[1]),
        pltpu.make_async_copy(sig.at[1], sigma_hbm.at[0, 0, 1], sem.at[2]),
    ]
    for copy in copies:
        copy.start()
    for copy in copies:
        copy.wait()


def shards(energies, green_free, coupling, screened, shift_offsets):
    orb = green_free.shape[-1]
    shifts = screened.shape[0]
    block = (2, orb, orb)
    hbm = pl.BlockSpec(memory_space=pltpu.HBM)
    vmem = pl.BlockSpec(memory_space=pltpu.VMEM)
    dma = pltpu.SemaphoreType.DMA
    half = jnp.bfloat16
    green, sigma = pl.pallas_call(
        functools.partial(kernel, energies),
        out_shape=(pltpu.VMEM(block, half), pltpu.VMEM(block, jnp.float32)),
        in_specs=[pl.BlockSpec(memory_space=pltpu.SMEM), hbm, hbm, hbm],
        out_specs=(vmem, vmem),
        scratch_shapes=[
            pltpu.VMEM(block, half),
            pltpu.VMEM(block, half),
            pltpu.VMEM((shifts, *block), half),
            pltpu.VMEM((3, *block), half),
            pltpu.VMEM((3, *block), half),
            *[pltpu.VMEM(block, half)] * 8,
            pltpu.VMEM((3, *block), jnp.float32),
            dma((2 + shifts,)),
            dma((7, CHUNKS)),
            dma((7, CHUNKS)),
        ],
        compiler_params=pltpu.CompilerParams(
            collective_id=0, has_side_effects=True, vmem_limit_bytes=57 * 2**20
        ),
    )(shift_offsets, green_free, coupling, screened)
    return pl.pallas_call(
        store,
        out_shape=(
            jax.ShapeDtypeStruct(green_free.shape, half),
            jax.ShapeDtypeStruct(green_free.shape, jnp.float32),
        ),
        in_specs=[vmem, vmem],
        out_specs=(hbm, hbm),
        scratch_shapes=[dma((3,))],
        compiler_params=pltpu.CompilerParams(vmem_limit_bytes=8 * 2**20),
    )(green, sigma)


def solution(mesh):
    placed = (
        P("energy", "slab", None, None, None),
        P("slab", None, None, None),
        P(None, "slab", None, None, None),
        P(),
    )
    return jax.shard_map(
        functools.partial(shards, mesh.shape["energy"]),
        mesh=mesh,
        in_specs=placed,
        out_specs=(P("energy", "slab", None, None, None), P("energy", "slab", None, None, None)),
        check_vma=False,
    )
```

```python
import functools

import jax
import jax.numpy as jnp
from jax import lax
from jax.experimental import pallas as pl
from jax.experimental.pallas import tpu as pltpu
from jax.sharding import PartitionSpec as P

MESH = pl.DeviceIdType.MESH
CHUNKS = 4
STEPS = 2
CHAIN, CROSS, BEYOND, NEAR, FAR, FREE_NEAR, FREE_FAR = range(7)
OWN, BESIDE, REMOTE = range(3)


def dot(a, b):
    return jnp.dot(a, b, preferred_element_type=jnp.float32)


def dot_t(a, b):
    return lax.dot_general(a, b, (((0,), (0,)), ((), ())), preferred_element_type=jnp.float32)


def complex_dot(first, second_re, second_im):
    half = first.shape[0] // 2
    by_re = dot(first, second_re)
    by_im = dot(first, second_im)
    return by_re[:half] - by_im[half:], by_im[:half] + by_re[half:]


def kernel(
    energies,
    shift_ref,
    free_hbm,
    coup_hbm,
    scr_hbm,
    green,
    sig,
    free,
    coup,
    scr,
    left,
    right,
    middle,
    chain_in,
    cross_in,
    beyond_in,
    near,
    far,
    free_near,
    free_far,
    weight,
    load_sem,
    send_sem,
    recv_sem,
    ready,
):
    e = lax.axis_index("energy")
    s = lax.axis_index("slab")
    shifts = scr.shape[0]
    orb = free.shape[1]
    rows = orb // CHUNKS
    parity = lax.rem(e, 2)
    partner = e + 1 - 2 * parity
    onward = lax.rem(e + 2 - 4 * parity + energies, energies)
    behind = lax.rem(e - 2 + 4 * parity + energies, energies)
    landing = (chain_in, cross_in, beyond_in, near, far, free_near, free_far)

    load_free = pltpu.make_async_copy(free_hbm.at[0, 0], free, load_sem.at[0])
    load_coup = pltpu.make_async_copy(coup_hbm.at[0], coup, load_sem.at[1])
    loads = [
        pltpu.make_async_copy(scr_hbm.at[k, 0], scr.at[k], load_sem.at[2 + k])
        for k in range(shifts)
    ]
    barrier = pltpu.get_barrier_semaphore()

    def greet(device):
        pl.semaphore_signal(barrier, inc=1, device_id=device, device_id_type=MESH)

    greet((partner, s))

    @pl.when(s == 1)
    def _():
        greet((e, 0))

    @pl.when(s == 2)
    def _():
        greet((partner, 1))
        greet((e, 3))

    @pl.when(s == 3)
    def _():
        greet((e, 2))

    far_side = jnp.where(s == 2, 3, s)

    @pl.when(onward > e)
    def _():
        greet((onward, far_side))

    @pl.when(jnp.logical_and(behind > e, s != 2))
    def _():
        greet((behind, s))

    @pl.when(jnp.logical_and(behind > e, s == 3))
    def _():
        greet((behind, 2))

    load_free.start()
    load_coup.start()

    def meet(row, senders):
        below = jnp.where(onward < e, 1, 0) + jnp.where(behind < e, senders, 0)
        pl.semaphore_wait(barrier, row + below)
        if senders:

            @pl.when(behind < e)
            def _():
                for sender in range(senders):
                    pl.semaphore_signal(
                        ready, inc=1, device_id=(behind, s - sender), device_id_type=MESH
                    )

    def meet_onward():
        @pl.when(onward > e)
        def _():
            pl.semaphore_wait(ready, 1)

    def load_screened():
        for load in loads:
            load.start()

    def move(kind, source, device, c):
        part = pl.ds(c * rows, rows)
        return pltpu.make_async_remote_copy(
            src_ref=source.at[:, part],
            dst_ref=landing[kind].at[:, part],
            send_sem=send_sem.at[kind, c],
            recv_sem=recv_sem.at[kind, c],
            device_id=device,
            device_id_type=MESH,
        )

    def arrived(kind, c):
        move(kind, free, (partner, s), c).wait_recv()

    def all_arrived(kind):
        for c in range(CHUNKS):
            arrived(kind, c)

    def sent(kind):
        for c in range(CHUNKS):
            move(kind, free, (partner, s), c).wait_send()

    def maps(block, slot):
        re, im = complex_dot(block[...].reshape(2 * orb, orb), coup[0], coup[1])
        left[slot, 0] = re.astype(jnp.bfloat16)
        left[slot, 1] = im.astype(jnp.bfloat16)
        re = dot_t(coup[0], block[0]) + dot_t(coup[1], block[1])
        im = dot_t(coup[0], block[1]) - dot_t(coup[1], block[0])
        right[slot, 0] = re.astype(jnp.bfloat16)
        right[slot, 1] = im.astype(jnp.bfloat16)

    def advance(slot, before, block, result, done=None):
        re, im = complex_dot(left[slot].reshape(2 * orb, orb), before[0], before[1])
        middle[0] = re.astype(jnp.bfloat16)
        middle[1] = im.astype(jnp.bfloat16)
        high = orb // STEPS
        for step in range(STEPS):
            part = pl.ds(step * high, high)
            stacked = middle[:, part, :].reshape(2 * high, orb)
            re, im = complex_dot(stacked, right[slot, 0], right[slot, 1])
            result[0, part, :] = (block[0, part, :].astype(jnp.float32) + re).astype(jnp.bfloat16)
            result[1, part, :] = (block[1, part, :].astype(jnp.float32) + im).astype(jnp.bfloat16)
            if done is not None:
                for c in range(step * CHUNKS // STEPS, (step + 1) * CHUNKS // STEPS):
                    done(c)

    def sum_weights():
        for load in loads:
            load.wait()
        near_shift = 2 * parity - 1

        @pl.loop(0, orb // 16)
        def _(step):
            part = pl.ds(pl.multiple_of(step * 16, 16), 16)
            total = [jnp.zeros((2, 16, orb), jnp.float32) for _ in range(3)]
            for k in range(shifts):
                block = scr[k, :, part, :].astype(jnp.float32)
                for slot, value in enumerate((0, near_shift, -near_shift)):
                    total[slot] = total[slot] + jnp.where(shift_ref[k] == value, block, 0.0)
            for slot in range(3):
                weight[slot, :, part, :] = total[slot]

    def term(block, slot, part):
        re = block[0, part, :].astype(jnp.float32)
        im = block[1, part, :].astype(jnp.float32)
        weight_re = weight[slot, 0, part, :]
        weight_im = weight[slot, 1, part, :]
        return re * weight_re - im * weight_im, re * weight_im + im * weight_re

    def begin_sigma(c):
        part = pl.ds(c * rows, rows)
        own = term(green, OWN, part)
        beside = term(near, BESIDE, part)
        sig[0, part, :] = -(own[1] + beside[1])
        sig[1, part, :] = own[0] + beside[0]

    def end_sigma(c):
        part = pl.ds(c * rows, rows)
        remote = term(far, REMOTE, part)
        sig[0, part, :] = sig[0, part, :] - remote[1]
        sig[1, part, :] = sig[1, part, :] + remote[0]

    @pl.when(s == 0)
    def _():
        load_free.wait()
        meet(2, 1)
        for c in range(CHUNKS):
            move(CHAIN, free, (e, 1), c).start()
        for c in range(CHUNKS):
            move(NEAR, free, (partner, s), c).start()
        load_screened()
        green[...] = free[...]
        sum_weights()
        meet_onward()
        for c in range(CHUNKS):
            arrived(NEAR, c)
            move(FAR, near, (onward, s), c).start()
            begin_sigma(c)
        for c in range(CHUNKS):
            arrived(FAR, c)
            end_sigma(c)
        load_coup.wait()
        sent(CHAIN)
        sent(NEAR)
        sent(FAR)

    @pl.when(s == 1)
    def _():
        load_free.wait()
        load_coup.wait()
        maps(free, OWN)
        meet(2, 1)
        all_arrived(CHAIN)
        advance(OWN, chain_in, free, green, lambda c: move(CROSS, green, (partner, 2), c).start())
        for c in range(CHUNKS):
            move(NEAR, green, (partner, s), c).start()
        load_screened()
        sum_weights()
        meet_onward()
        for c in range(CHUNKS):
            arrived(NEAR, c)
            move(CHAIN, near, (partner, 2), c).start()
            move(FAR, near, (onward, s), c).start()
            begin_sigma(c)
        for c in range(CHUNKS):
            arrived(FAR, c)
            end_sigma(c)
        sent(CROSS)
        sent(NEAR)
        sent(CHAIN)
        sent(FAR)

    @pl.when(s == 2)
    def _():
        load_free.wait()
        meet(2, 0)
        for c in range(CHUNKS):
            move(FREE_NEAR, free, (partner, s), c).start()
        load_coup.wait()
        load_screened()
        maps(free, OWN)
        sum_weights()
        all_arrived(FREE_NEAR)
        maps(free_near, BESIDE)
        meet_onward()
        all_arrived(CROSS)

        def hand_on(c):
            move(BEYOND, near, (onward, 3), c).start()
            move(CROSS, near, (e, 3), c).start()

        advance(BESIDE, cross_in, free_near, near, hand_on)
        all_arrived(CHAIN)
        advance(OWN, chain_in, free, green, lambda c: move(CHAIN, green, (e, 3), c).start())
        for c in range(CHUNKS):
            begin_sigma(c)
        for c in range(CHUNKS):
            arrived(FAR, c)
            end_sigma(c)
        sent(FREE_NEAR)
        sent(BEYOND)
        sent(CROSS)
        sent(CHAIN)

    @pl.when(s == 3)
    def _():
        load_free.wait()
        load_coup.wait()
        load_screened()
        maps(free, OWN)
        sum_weights()
        meet(2, 2)
        for c in range(CHUNKS):
            move(FREE_NEAR, free, (partner, s), c).start()
        meet_onward()
        for c in range(CHUNKS):
            arrived(FREE_NEAR, c)
            move(FREE_FAR, free_near, (onward, s), c).start()
        maps(free_near, BESIDE)
        all_arrived(CROSS)
        advance(BESIDE, cross_in, free_near, near)
        all_arrived(FREE_FAR)
        maps(free_far, REMOTE)
        all_arrived(CHAIN)
        advance(OWN, chain_in, free, green)
        for c in range(CHUNKS):
            begin_sigma(c)
        for c in range(CHUNKS):
            arrived(BEYOND, c)
            move(FAR, beyond_in, (e, 2), c).start()
        advance(REMOTE, beyond_in, free_far, far, end_sigma)
        sent(FREE_NEAR)
        sent(FREE_FAR)
        sent(FAR)


def store(green, sig, green_hbm, sigma_hbm, sem):
    copies = [
        pltpu.make_async_copy(green, green_hbm.at[0, 0], sem.at[0]),
        pltpu.make_async_copy(sig.at[0], sigma_hbm.at[0, 0, 0], sem.at[1]),
        pltpu.make_async_copy(sig.at[1], sigma_hbm.at[0, 0, 1], sem.at[2]),
    ]
    for copy in copies:
        copy.start()
    for copy in copies:
        copy.wait()


def shards(energies, green_free, coupling, screened, shift_offsets):
    orb = green_free.shape[-1]
    shifts = screened.shape[0]
    block = (2, orb, orb)
    hbm = pl.BlockSpec(memory_space=pltpu.HBM)
    vmem = pl.BlockSpec(memory_space=pltpu.VMEM)
    dma = pltpu.SemaphoreType.DMA
    half = jnp.bfloat16
    green, sigma = pl.pallas_call(
        functools.partial(kernel, energies),
        out_shape=(pltpu.VMEM(block, half), pltpu.VMEM(block, jnp.float32)),
        in_specs=[pl.BlockSpec(memory_space=pltpu.SMEM), hbm, hbm, hbm],
        out_specs=(vmem, vmem),
        scratch_shapes=[
            pltpu.VMEM(block, half),
            pltpu.VMEM(block, half),
            pltpu.VMEM((shifts, *block), half),
            pltpu.VMEM((3, *block), half),
            pltpu.VMEM((3, *block), half),
            *[pltpu.VMEM(block, half)] * 8,
            pltpu.VMEM((3, *block), jnp.float32),
            dma((2 + shifts,)),
            dma((7, CHUNKS)),
            dma((7, CHUNKS)),
            pltpu.SemaphoreType.REGULAR,
        ],
        compiler_params=pltpu.CompilerParams(
            collective_id=0, has_side_effects=True, vmem_limit_bytes=57 * 2**20
        ),
    )(shift_offsets, green_free, coupling, screened)
    return pl.pallas_call(
        store,
        out_shape=(
            jax.ShapeDtypeStruct(green_free.shape, half),
            jax.ShapeDtypeStruct(green_free.shape, jnp.float32),
        ),
        in_specs=[vmem, vmem],
        out_specs=(hbm, hbm),
        scratch_shapes=[dma((3,))],
        compiler_params=pltpu.CompilerParams(vmem_limit_bytes=8 * 2**20),
    )(green, sigma)


def solution(mesh):
    placed = (
        P("energy", "slab", None, None, None),
        P("slab", None, None, None),
        P(None, "slab", None, None, None),
        P(),
    )
    return jax.shard_map(
        functools.partial(shards, mesh.shape["energy"]),
        mesh=mesh,
        in_specs=placed,
        out_specs=(P("energy", "slab", None, None, None), P("energy", "slab", None, None, None)),
        check_vma=False,
    )
```

```python
import functools

import jax
import jax.numpy as jnp
from jax import lax
from jax.experimental import pallas as pl
from jax.experimental.pallas import tpu as pltpu
from jax.sharding import PartitionSpec as P

MESH = pl.DeviceIdType.MESH
CHUNKS = 4
STEPS = 2
CHAIN, CROSS, BEYOND, NEAR, FAR, FREE_NEAR, FREE_FAR, WRAP, WRAP_TWO = range(9)
OWN, BESIDE, REMOTE = range(3)


def dot(a, b):
    return jnp.dot(a, b, preferred_element_type=jnp.float32)


def dot_t(a, b):
    return lax.dot_general(a, b, (((0,), (0,)), ((), ())), preferred_element_type=jnp.float32)


def complex_dot(first, second_re, second_im):
    half = first.shape[0] // 2
    by_re = dot(first, second_re)
    by_im = dot(first, second_im)
    return by_re[:half] - by_im[half:], by_im[:half] + by_re[half:]


def kernel(
    energies,
    shift_ref,
    free_hbm,
    coup_hbm,
    scr_hbm,
    green,
    sig,
    free,
    coup,
    scr,
    left,
    right,
    middle,
    chain_in,
    cross_in,
    beyond_in,
    near,
    far,
    free_near,
    free_far,
    weight,
    load_sem,
    send_sem,
    recv_sem,
    ready,
    near_ready,
):
    e = lax.axis_index("energy")
    s = lax.axis_index("slab")
    shifts = scr.shape[0]
    orb = free.shape[1]
    rows = orb // CHUNKS
    parity = lax.rem(e, 2)
    partner = e + 1 - 2 * parity
    onward = lax.rem(e + 2 - 4 * parity + energies, energies)
    behind = lax.rem(e - 2 + 4 * parity + energies, energies)
    landing = (chain_in, cross_in, beyond_in, near, far, free_near, free_far)

    load_free = pltpu.make_async_copy(free_hbm.at[0, 0], free, load_sem.at[0])
    load_coup = pltpu.make_async_copy(coup_hbm.at[0], coup, load_sem.at[1])
    loads = [
        pltpu.make_async_copy(scr_hbm.at[k, 0], scr.at[k], load_sem.at[2 + k])
        for k in range(shifts)
    ]
    barrier = pltpu.get_barrier_semaphore()

    def greet(device):
        pl.semaphore_signal(barrier, inc=1, device_id=device, device_id_type=MESH)

    last = energies - 1
    is_first = e == 0
    is_last = e == last
    has_onward = e != last - 1
    far_side = jnp.where(s == 2, 3, s)

    @pl.when(jnp.logical_or(e > 0, s > 0))
    def _():
        greet((partner, s))

    @pl.when(s == 1)
    def _():
        greet((e, 0))

    @pl.when(s == 2)
    def _():
        greet((partner, 1))
        greet((e, 3))

    @pl.when(s == 3)
    def _():
        greet((e, 2))

    @pl.when(onward > e)
    def _():
        greet((onward, far_side))

    @pl.when(jnp.logical_and(e > 0, jnp.logical_and(behind > e, s != 2)))
    def _():
        greet((behind, s))

    @pl.when(jnp.logical_and(e > 0, jnp.logical_and(behind > e, s == 3)))
    def _():
        greet((behind, 2))

    @pl.when(is_first)
    def _():
        greet((last, s))

    @pl.when(jnp.logical_and(is_first, s == 2))
    def _():
        greet((last, 1))

    load_free.start()
    load_coup.start()

    def meet(row, senders, wrapped):
        below = jnp.where(jnp.logical_and(has_onward, onward < e), 1, 0)
        below = below + jnp.where(behind < e, senders, 0) + jnp.where(is_last, wrapped, 0)
        pl.semaphore_wait(barrier, row + below)
        if senders:

            @pl.when(behind < e)
            def _():
                for sender in range(senders):
                    pl.semaphore_signal(
                        ready, inc=1, device_id=(behind, s - sender), device_id_type=MESH
                    )

    def meet_onward():
        @pl.when(onward > e)
        def _():
            pl.semaphore_wait(ready, 1)

    def load_screened():
        for load in loads:
            load.start()

    def move(kind, source, device, c, sender=None):
        sender = kind if sender is None else sender
        part = pl.ds(c * rows, rows)
        return pltpu.make_async_remote_copy(
            src_ref=source.at[:, part],
            dst_ref=landing[kind].at[:, part],
            send_sem=send_sem.at[sender, c],
            recv_sem=recv_sem.at[kind, c],
            device_id=device,
            device_id_type=MESH,
        )

    def arrived(kind, c):
        move(kind, free, (partner, s), c).wait_recv()

    def all_arrived(kind):
        for c in range(CHUNKS):
            arrived(kind, c)

    def sent(kind):
        for c in range(CHUNKS):
            move(0, free, (partner, s), c, kind).wait_send()

    def maps(block, slot):
        re, im = complex_dot(block[...].reshape(2 * orb, orb), coup[0], coup[1])
        left[slot, 0] = re.astype(jnp.bfloat16)
        left[slot, 1] = im.astype(jnp.bfloat16)
        re = dot_t(coup[0], block[0]) + dot_t(coup[1], block[1])
        im = dot_t(coup[0], block[1]) - dot_t(coup[1], block[0])
        right[slot, 0] = re.astype(jnp.bfloat16)
        right[slot, 1] = im.astype(jnp.bfloat16)

    def advance(slot, before, block, result, done=None):
        re, im = complex_dot(left[slot].reshape(2 * orb, orb), before[0], before[1])
        middle[0] = re.astype(jnp.bfloat16)
        middle[1] = im.astype(jnp.bfloat16)
        high = orb // STEPS
        for step in range(STEPS):
            part = pl.ds(step * high, high)
            stacked = middle[:, part, :].reshape(2 * high, orb)
            re, im = complex_dot(stacked, right[slot, 0], right[slot, 1])
            result[0, part, :] = (block[0, part, :].astype(jnp.float32) + re).astype(jnp.bfloat16)
            result[1, part, :] = (block[1, part, :].astype(jnp.float32) + im).astype(jnp.bfloat16)
            if done is not None:
                for c in range(step * CHUNKS // STEPS, (step + 1) * CHUNKS // STEPS):
                    done(c)

    def sum_weights():
        for load in loads:
            load.wait()
        near_shift = 2 * parity - 1

        @pl.loop(0, orb // 16)
        def _(step):
            part = pl.ds(pl.multiple_of(step * 16, 16), 16)
            total = [jnp.zeros((2, 16, orb), jnp.float32) for _ in range(3)]
            for k in range(shifts):
                block = scr[k, :, part, :].astype(jnp.float32)
                for slot, value in enumerate((0, near_shift, -near_shift)):
                    total[slot] = total[slot] + jnp.where(shift_ref[k] == value, block, 0.0)
            for slot in range(3):
                weight[slot, :, part, :] = total[slot]

    def term(block, slot, part):
        re = block[0, part, :].astype(jnp.float32)
        im = block[1, part, :].astype(jnp.float32)
        weight_re = weight[slot, 0, part, :]
        weight_im = weight[slot, 1, part, :]
        return re * weight_re - im * weight_im, re * weight_im + im * weight_re

    def begin_sigma(c):
        part = pl.ds(c * rows, rows)
        own = term(green, OWN, part)
        beside = term(near, BESIDE, part)
        sig[0, part, :] = -(own[1] + beside[1])
        sig[1, part, :] = own[0] + beside[0]

    def end_sigma(c):
        part = pl.ds(c * rows, rows)
        remote = term(far, REMOTE, part)
        sig[0, part, :] = sig[0, part, :] - remote[1]
        sig[1, part, :] = sig[1, part, :] + remote[0]

    @pl.when(s == 0)
    def _():
        load_free.wait()
        meet(jnp.where(e == 1, 1, 2), 1, 1)
        for c in range(CHUNKS):
            move(CHAIN, free, (e, 1), c).start()

        @pl.when(is_last)
        def _():
            for c in range(CHUNKS):
                move(FAR, free, (0, s), c, WRAP).start()
            sent(WRAP)

        @pl.when(is_first)
        def _():
            pl.semaphore_signal(near_ready, inc=1, device_id=(1, 0), device_id_type=MESH)

        @pl.when(e == 1)
        def _():
            pl.semaphore_wait(near_ready, 1)

        for c in range(CHUNKS):
            move(NEAR, free, (partner, s), c).start()
        load_screened()
        green[...] = free[...]
        sum_weights()
        meet_onward()
        for c in range(CHUNKS):
            arrived(NEAR, c)

            @pl.when(has_onward)
            def _():
                move(FAR, near, (onward, s), c).start()

            begin_sigma(c)
        for c in range(CHUNKS):
            arrived(FAR, c)
            end_sigma(c)
        load_coup.wait()
        sent(CHAIN)
        sent(NEAR)

        @pl.when(has_onward)
        def _():
            sent(FAR)

    @pl.when(s == 1)
    def _():
        def relay(c):
            arrived(NEAR, c)
            move(CHAIN, near, (partner, 2), c).start()

        load_free.wait()
        load_coup.wait()
        maps(free, OWN)
        meet(2, 1, 2)

        @pl.when(is_first)
        def _():
            for c in range(CHUNKS):
                relay(c)

        all_arrived(CHAIN)

        def hand_on(c):
            @pl.when(is_last)
            def _():
                move(BEYOND, green, (0, 2), c, WRAP).start()

            @pl.when(jnp.logical_not(is_last))
            def _():
                move(CROSS, green, (partner, 2), c).start()

        advance(OWN, chain_in, free, green, hand_on)

        @pl.when(is_last)
        def _():
            for c in range(CHUNKS):
                move(FAR, green, (0, 1), c, WRAP_TWO).start()
            sent(WRAP)
            for c in range(CHUNKS):
                move(CROSS, green, (partner, 2), c).start()
            sent(WRAP_TWO)

        for c in range(CHUNKS):
            move(NEAR, green, (partner, s), c).start()
        load_screened()
        sum_weights()

        @pl.when(e > 0)
        def _():
            for c in range(CHUNKS):
                relay(c)

        meet_onward()
        for c in range(CHUNKS):

            @pl.when(has_onward)
            def _():
                move(FAR, near, (onward, s), c).start()

            begin_sigma(c)
        for c in range(CHUNKS):
            arrived(FAR, c)
            end_sigma(c)
        sent(CROSS)
        sent(NEAR)
        sent(CHAIN)

        @pl.when(has_onward)
        def _():
            sent(FAR)

    @pl.when(s == 2)
    def _():
        load_free.wait()
        meet(2, 0, 1)

        @pl.when(is_last)
        def _():
            for c in range(CHUNKS):
                move(FREE_FAR, free, (0, 2), c, WRAP).start()

        for c in range(CHUNKS):
            move(FREE_NEAR, free, (partner, s), c).start()
        load_coup.wait()
        load_screened()
        maps(free, OWN)
        sum_weights()
        all_arrived(FREE_NEAR)
        maps(free_near, BESIDE)
        all_arrived(CROSS)
        advance(BESIDE, cross_in, free_near, near, lambda c: move(CROSS, near, (e, 3), c).start())
        meet_onward()

        @pl.when(has_onward)
        def _():
            for c in range(CHUNKS):
                move(BEYOND, near, (onward, 3), c).start()

        all_arrived(CHAIN)
        advance(OWN, chain_in, free, green, lambda c: move(CHAIN, green, (e, 3), c).start())
        for c in range(CHUNKS):
            begin_sigma(c)

        @pl.when(is_first)
        def _():
            all_arrived(FREE_FAR)
            maps(free_far, REMOTE)
            all_arrived(BEYOND)
            advance(
                REMOTE,
                beyond_in,
                free_far,
                far,
                lambda c: move(BEYOND, far, (e, 3), c, WRAP).start(),
            )

        @pl.when(e > 0)
        def _():
            all_arrived(FAR)

        for c in range(CHUNKS):
            end_sigma(c)
        sent(FREE_NEAR)
        sent(CROSS)
        sent(CHAIN)

        @pl.when(has_onward)
        def _():
            sent(BEYOND)

        @pl.when(jnp.logical_or(is_first, is_last))
        def _():
            sent(WRAP)

    @pl.when(s == 3)
    def _():
        load_free.wait()
        load_coup.wait()
        load_screened()
        maps(free, OWN)
        sum_weights()
        meet(2, 2, 1)

        @pl.when(is_last)
        def _():
            for c in range(CHUNKS):
                move(FREE_FAR, free, (0, 3), c, WRAP).start()
            sent(WRAP)

        for c in range(CHUNKS):
            move(FREE_NEAR, free, (partner, s), c).start()
        meet_onward()
        for c in range(CHUNKS):
            arrived(FREE_NEAR, c)

            @pl.when(has_onward)
            def _():
                move(FREE_FAR, free_near, (onward, s), c).start()

        maps(free_near, BESIDE)
        all_arrived(CROSS)
        advance(BESIDE, cross_in, free_near, near)

        @pl.when(e > 0)
        def _():
            all_arrived(FREE_FAR)
            maps(free_far, REMOTE)

        all_arrived(CHAIN)
        advance(OWN, chain_in, free, green)
        for c in range(CHUNKS):
            begin_sigma(c)

        @pl.when(is_first)
        def _():
            all_arrived(FREE_FAR)
            maps(free_far, REMOTE)

        for c in range(CHUNKS):
            arrived(BEYOND, c)

            @pl.when(e > 0)
            def _():
                move(FAR, beyond_in, (e, 2), c).start()

        advance(REMOTE, beyond_in, free_far, far, end_sigma)
        sent(FREE_NEAR)

        @pl.when(has_onward)
        def _():
            sent(FREE_FAR)

        @pl.when(e > 0)
        def _():
            sent(FAR)


def store(green, sig, green_hbm, sigma_hbm, sem):
    copies = [
        pltpu.make_async_copy(green, green_hbm.at[0, 0], sem.at[0]),
        pltpu.make_async_copy(sig.at[0], sigma_hbm.at[0, 0, 0], sem.at[1]),
        pltpu.make_async_copy(sig.at[1], sigma_hbm.at[0, 0, 1], sem.at[2]),
    ]
    for copy in copies:
        copy.start()
    for copy in copies:
        copy.wait()


def shards(energies, green_free, coupling, screened, shift_offsets):
    orb = green_free.shape[-1]
    shifts = screened.shape[0]
    block = (2, orb, orb)
    hbm = pl.BlockSpec(memory_space=pltpu.HBM)
    vmem = pl.BlockSpec(memory_space=pltpu.VMEM)
    dma = pltpu.SemaphoreType.DMA
    half = jnp.bfloat16
    green, sigma = pl.pallas_call(
        functools.partial(kernel, energies),
        out_shape=(pltpu.VMEM(block, half), pltpu.VMEM(block, jnp.float32)),
        in_specs=[pl.BlockSpec(memory_space=pltpu.SMEM), hbm, hbm, hbm],
        out_specs=(vmem, vmem),
        scratch_shapes=[
            pltpu.VMEM(block, half),
            pltpu.VMEM(block, half),
            pltpu.VMEM((shifts, *block), half),
            pltpu.VMEM((3, *block), half),
            pltpu.VMEM((3, *block), half),
            *[pltpu.VMEM(block, half)] * 8,
            pltpu.VMEM((3, *block), jnp.float32),
            dma((2 + shifts,)),
            dma((9, CHUNKS)),
            dma((7, CHUNKS)),
            pltpu.SemaphoreType.REGULAR,
            pltpu.SemaphoreType.REGULAR,
        ],
        compiler_params=pltpu.CompilerParams(
            collective_id=0, has_side_effects=True, vmem_limit_bytes=57 * 2**20
        ),
    )(shift_offsets, green_free, coupling, screened)
    return pl.pallas_call(
        store,
        out_shape=(
            jax.ShapeDtypeStruct(green_free.shape, half),
            jax.ShapeDtypeStruct(green_free.shape, jnp.float32),
        ),
        in_specs=[vmem, vmem],
        out_specs=(hbm, hbm),
        scratch_shapes=[dma((3,))],
        compiler_params=pltpu.CompilerParams(vmem_limit_bytes=8 * 2**20),
    )(green, sigma)


def solution(mesh):
    placed = (
        P("energy", "slab", None, None, None),
        P("slab", None, None, None),
        P(None, "slab", None, None, None),
        P(),
    )
    return jax.shard_map(
        functools.partial(shards, mesh.shape["energy"]),
        mesh=mesh,
        in_specs=placed,
        out_specs=(P("energy", "slab", None, None, None), P("energy", "slab", None, None, None)),
        check_vma=False,
    )
```

```python
import functools

import jax
import jax.numpy as jnp
from jax import lax
from jax.experimental import pallas as pl
from jax.experimental.pallas import tpu as pltpu
from jax.sharding import PartitionSpec as P

MESH = pl.DeviceIdType.MESH
CHUNKS = 4
STEPS = 2
CHAIN, CROSS, BEYOND, NEAR, FAR, FREE_NEAR, FREE_FAR, SEAM, WRAP, WRAP_TWO = range(10)
OWN, BESIDE, REMOTE = range(3)


def dot(a, b):
    return jnp.dot(a, b, preferred_element_type=jnp.float32)


def dot_t(a, b):
    return lax.dot_general(a, b, (((0,), (0,)), ((), ())), preferred_element_type=jnp.float32)


def complex_dot(first, second_re, second_im):
    half = first.shape[0] // 2
    by_re = dot(first, second_re)
    by_im = dot(first, second_im)
    return by_re[:half] - by_im[half:], by_im[:half] + by_re[half:]


def kernel(
    energies,
    shift_ref,
    free_hbm,
    coup_hbm,
    scr_hbm,
    green,
    sig,
    free,
    coup,
    scr,
    left,
    right,
    middle,
    chain_in,
    cross_in,
    beyond_in,
    near,
    far,
    free_near,
    free_far,
    seam_in,
    weight,
    load_sem,
    send_sem,
    recv_sem,
    ready,
    near_ready,
):
    e = lax.axis_index("energy")
    s = lax.axis_index("slab")
    shifts = scr.shape[0]
    orb = free.shape[1]
    rows = orb // CHUNKS
    parity = lax.rem(e, 2)
    partner = e + 1 - 2 * parity
    onward = lax.rem(e + 2 - 4 * parity + energies, energies)
    behind = lax.rem(e - 2 + 4 * parity + energies, energies)
    landing = (chain_in, cross_in, beyond_in, near, far, free_near, free_far, seam_in)

    load_free = pltpu.make_async_copy(free_hbm.at[0, 0], free, load_sem.at[0])
    load_coup = pltpu.make_async_copy(coup_hbm.at[0], coup, load_sem.at[1])
    loads = [
        pltpu.make_async_copy(scr_hbm.at[k, 0], scr.at[k], load_sem.at[2 + k])
        for k in range(shifts)
    ]
    barrier = pltpu.get_barrier_semaphore()

    def greet(device):
        pl.semaphore_signal(barrier, inc=1, device_id=device, device_id_type=MESH)

    last = energies - 1
    is_first = e == 0
    is_last = e == last
    has_onward = e != last - 1
    far_side = jnp.where(s == 2, 3, s)

    lead = jnp.logical_and(is_last, s == 0)

    @pl.when(jnp.logical_or(s > 0, jnp.logical_and(e > 0, has_onward)))
    def _():
        greet((partner, s))

    @pl.when(s == 1)
    def _():
        greet((e, 0))

    @pl.when(s == 2)
    def _():
        greet((partner, 1))
        greet((e, 3))

    @pl.when(s == 3)
    def _():
        greet((e, 2))

    @pl.when(jnp.logical_or(onward > e, lead))
    def _():
        greet((onward, far_side))

    led = jnp.logical_and(e == last - 2, s == 0)
    greets_behind = jnp.logical_and(behind > e, jnp.logical_not(led))

    @pl.when(jnp.logical_and(e > 0, jnp.logical_and(greets_behind, s != 2)))
    def _():
        greet((behind, s))

    @pl.when(jnp.logical_and(e > 0, jnp.logical_and(behind > e, s == 3)))
    def _():
        greet((behind, 2))

    @pl.when(jnp.logical_and(is_first, s < 3))
    def _():
        greet((last, jnp.where(s == 2, 2, 0)))

    @pl.when(jnp.logical_and(is_last, s == 0))
    def _():
        greet((last, 1))

    @pl.when(jnp.logical_and(is_first, s == 2))
    def _():
        greet((last, 1))

    load_free.start()
    load_coup.start()

    def meet(row, senders, wrapped):
        waits = jnp.logical_and(has_onward, jnp.logical_and(onward < e, jnp.logical_not(lead)))
        answers = jnp.logical_or(behind < e, led)
        below = jnp.where(waits, 1, 0) + jnp.where(is_last, wrapped, 0)
        below = below + jnp.where(answers, senders, 0)
        pl.semaphore_wait(barrier, row + below)
        if senders:

            @pl.when(answers)
            def _():
                for sender in range(senders):
                    pl.semaphore_signal(
                        ready, inc=1, device_id=(behind, s - sender), device_id_type=MESH
                    )

    def meet_onward():
        @pl.when(jnp.logical_or(onward > e, lead))
        def _():
            pl.semaphore_wait(ready, 1)

    def load_screened():
        for load in loads:
            load.start()

    def move(kind, source, device, c, sender=None):
        sender = kind if sender is None else sender
        part = pl.ds(c * rows, rows)
        return pltpu.make_async_remote_copy(
            src_ref=source.at[:, part],
            dst_ref=landing[kind].at[:, part],
            send_sem=send_sem.at[sender, c],
            recv_sem=recv_sem.at[kind, c],
            device_id=device,
            device_id_type=MESH,
        )

    def arrived(kind, c):
        move(kind, free, (partner, s), c).wait_recv()

    def all_arrived(kind):
        for c in range(CHUNKS):
            arrived(kind, c)

    def sent(kind):
        for c in range(CHUNKS):
            move(0, free, (partner, s), c, kind).wait_send()

    def maps(block, slot):
        re, im = complex_dot(block[...].reshape(2 * orb, orb), coup[0], coup[1])
        left[slot, 0] = re.astype(jnp.bfloat16)
        left[slot, 1] = im.astype(jnp.bfloat16)
        re = dot_t(coup[0], block[0]) + dot_t(coup[1], block[1])
        im = dot_t(coup[0], block[1]) - dot_t(coup[1], block[0])
        right[slot, 0] = re.astype(jnp.bfloat16)
        right[slot, 1] = im.astype(jnp.bfloat16)

    def advance(slot, before, block, result, done=None):
        re, im = complex_dot(left[slot].reshape(2 * orb, orb), before[0], before[1])
        middle[0] = re.astype(jnp.bfloat16)
        middle[1] = im.astype(jnp.bfloat16)
        high = orb // STEPS
        for step in range(STEPS):
            part = pl.ds(step * high, high)
            stacked = middle[:, part, :].reshape(2 * high, orb)
            re, im = complex_dot(stacked, right[slot, 0], right[slot, 1])
            result[0, part, :] = (block[0, part, :].astype(jnp.float32) + re).astype(jnp.bfloat16)
            result[1, part, :] = (block[1, part, :].astype(jnp.float32) + im).astype(jnp.bfloat16)
            if done is not None:
                for c in range(step * CHUNKS // STEPS, (step + 1) * CHUNKS // STEPS):
                    done(c)

    def sum_weights():
        for load in loads:
            load.wait()
        near_shift = 2 * parity - 1

        @pl.loop(0, orb // 16)
        def _(step):
            part = pl.ds(pl.multiple_of(step * 16, 16), 16)
            total = [jnp.zeros((2, 16, orb), jnp.float32) for _ in range(3)]
            for k in range(shifts):
                block = scr[k, :, part, :].astype(jnp.float32)
                for slot, value in enumerate((0, near_shift, -near_shift)):
                    total[slot] = total[slot] + jnp.where(shift_ref[k] == value, block, 0.0)
            for slot in range(3):
                weight[slot, :, part, :] = total[slot]

    def term(block, slot, part):
        re = block[0, part, :].astype(jnp.float32)
        im = block[1, part, :].astype(jnp.float32)
        weight_re = weight[slot, 0, part, :]
        weight_im = weight[slot, 1, part, :]
        return re * weight_re - im * weight_im, re * weight_im + im * weight_re

    def begin_sigma(c):
        part = pl.ds(c * rows, rows)
        own = term(green, OWN, part)
        beside = term(near, BESIDE, part)
        sig[0, part, :] = -(own[1] + beside[1])
        sig[1, part, :] = own[0] + beside[0]

    def end_sigma(c):
        part = pl.ds(c * rows, rows)
        remote = term(far, REMOTE, part)
        sig[0, part, :] = sig[0, part, :] - remote[1]
        sig[1, part, :] = sig[1, part, :] + remote[0]

    @pl.when(s == 0)
    def _():
        meet(jnp.where(jnp.logical_or(e == 1, is_last), 1, 2), 1, 2)
        for c in range(CHUNKS):
            move(CHAIN, free_hbm.at[0, 0], (e, 1), c).start()
        load_free.wait()

        @pl.when(is_last)
        def _():
            for c in range(CHUNKS):
                move(FAR, free, (0, s), c, WRAP).start()
            for c in range(CHUNKS):
                arrived(SEAM, c)
                move(FAR, seam_in, (0, 1), c, WRAP_TWO).start()

        @pl.when(jnp.logical_or(is_first, e == last - 1))
        def _():
            pl.semaphore_signal(near_ready, inc=1, device_id=(partner, 0), device_id_type=MESH)

        @pl.when(e == 1)
        def _():
            pl.semaphore_wait(near_ready, 1)

        @pl.when(jnp.logical_not(is_last))
        def _():
            for c in range(CHUNKS):
                move(NEAR, free, (partner, s), c).start()

        load_screened()
        green[...] = free[...]
        sum_weights()
        meet_onward()
        for c in range(CHUNKS):
            arrived(NEAR, c)

            @pl.when(has_onward)
            def _():
                move(FAR, near, (onward, s), c).start()

            begin_sigma(c)

        @pl.when(is_last)
        def _():
            pl.semaphore_wait(near_ready, 1)
            for c in range(CHUNKS):
                move(NEAR, free, (partner, s), c).start()

        for c in range(CHUNKS):
            arrived(FAR, c)
            end_sigma(c)
        load_coup.wait()
        sent(CHAIN)
        sent(NEAR)

        @pl.when(is_last)
        def _():
            sent(WRAP)
            sent(WRAP_TWO)

        @pl.when(has_onward)
        def _():
            sent(FAR)

    @pl.when(s == 1)
    def _():
        def relay(c):
            arrived(NEAR, c)
            move(CHAIN, near, (partner, 2), c).start()

        load_free.wait()
        load_coup.wait()
        maps(free, OWN)
        meet(2, 1, 2)

        @pl.when(is_first)
        def _():
            for c in range(CHUNKS):
                relay(c)

        all_arrived(CHAIN)

        def hand_on(c):
            @pl.when(is_last)
            def _():
                move(BEYOND, green, (0, 2), c, WRAP).start()

            @pl.when(jnp.logical_not(is_last))
            def _():
                move(CROSS, green, (partner, 2), c).start()

        advance(OWN, chain_in, free, green, hand_on)

        @pl.when(is_last)
        def _():
            for c in range(CHUNKS):
                move(SEAM, green, (e, 0), c).start()
            sent(WRAP)
            for c in range(CHUNKS):
                move(CROSS, green, (partner, 2), c).start()
            sent(SEAM)

        for c in range(CHUNKS):
            move(NEAR, green, (partner, s), c).start()
        load_screened()
        sum_weights()

        @pl.when(e > 0)
        def _():
            for c in range(CHUNKS):
                relay(c)

        meet_onward()
        for c in range(CHUNKS):

            @pl.when(has_onward)
            def _():
                move(FAR, near, (onward, s), c).start()

            begin_sigma(c)
        for c in range(CHUNKS):
            arrived(FAR, c)
            end_sigma(c)
        sent(CROSS)
        sent(NEAR)
        sent(CHAIN)

        @pl.when(has_onward)
        def _():
            sent(FAR)

    @pl.when(s == 2)
    def _():
        load_free.wait()
        meet(2, 0, 1)

        @pl.when(is_last)
        def _():
            for c in range(CHUNKS):
                move(FREE_FAR, free, (0, 2), c, WRAP).start()
            sent(WRAP)

        for c in range(CHUNKS):
            move(FREE_NEAR, free, (partner, s), c).start()
        load_coup.wait()
        load_screened()
        maps(free, OWN)
        sum_weights()
        all_arrived(FREE_NEAR)
        maps(free_near, BESIDE)
        all_arrived(CROSS)
        advance(BESIDE, cross_in, free_near, near, lambda c: move(CROSS, near, (e, 3), c).start())
        meet_onward()

        @pl.when(has_onward)
        def _():
            for c in range(CHUNKS):
                move(BEYOND, near, (onward, 3), c).start()

        all_arrived(CHAIN)
        advance(OWN, chain_in, free, green, lambda c: move(CHAIN, green, (e, 3), c).start())
        for c in range(CHUNKS):
            begin_sigma(c)

        @pl.when(is_first)
        def _():
            all_arrived(FREE_FAR)
            maps(free_far, REMOTE)
            all_arrived(BEYOND)
            advance(
                REMOTE,
                beyond_in,
                free_far,
                far,
                lambda c: move(BEYOND, far, (e, 3), c, WRAP).start(),
            )

        @pl.when(e > 0)
        def _():
            all_arrived(FAR)

        for c in range(CHUNKS):
            end_sigma(c)
        sent(FREE_NEAR)
        sent(CROSS)
        sent(CHAIN)

        @pl.when(has_onward)
        def _():
            sent(BEYOND)

        @pl.when(is_first)
        def _():
            sent(WRAP)

    @pl.when(s == 3)
    def _():
        load_free.wait()
        load_coup.wait()
        load_screened()
        meet(2, 2, 0)

        @pl.when(is_last)
        def _():
            for c in range(CHUNKS):
                move(SEAM, free, (1, 3), c).start()

        maps(free, OWN)
        sum_weights()

        @pl.when(is_last)
        def _():
            sent(SEAM)

        for c in range(CHUNKS):
            move(FREE_NEAR, free, (partner, s), c).start()
        meet_onward()
        for c in range(CHUNKS):
            arrived(FREE_NEAR, c)

            @pl.when(has_onward)
            def _():
                move(FREE_FAR, free_near, (onward, s), c).start()

        maps(free_near, BESIDE)
        all_arrived(CROSS)
        advance(BESIDE, cross_in, free_near, near)

        @pl.when(e > 0)
        def _():
            all_arrived(FREE_FAR)
            maps(free_far, REMOTE)

        all_arrived(CHAIN)
        advance(OWN, chain_in, free, green)

        @pl.when(e == 1)
        def _():
            for c in range(CHUNKS):
                arrived(SEAM, c)
                move(FREE_FAR, seam_in, (0, 3), c, WRAP).start()

        for c in range(CHUNKS):
            begin_sigma(c)

        @pl.when(is_first)
        def _():
            all_arrived(FREE_FAR)
            maps(free_far, REMOTE)

        for c in range(CHUNKS):
            arrived(BEYOND, c)

            @pl.when(e > 0)
            def _():
                move(FAR, beyond_in, (e, 2), c).start()

        advance(REMOTE, beyond_in, free_far, far, end_sigma)
        sent(FREE_NEAR)

        @pl.when(e == 1)
        def _():
            sent(WRAP)

        @pl.when(has_onward)
        def _():
            sent(FREE_FAR)

        @pl.when(e > 0)
        def _():
            sent(FAR)


def store(green, sig, green_hbm, sigma_hbm, sem):
    copies = [
        pltpu.make_async_copy(green, green_hbm.at[0, 0], sem.at[0]),
        pltpu.make_async_copy(sig.at[0], sigma_hbm.at[0, 0, 0], sem.at[1]),
        pltpu.make_async_copy(sig.at[1], sigma_hbm.at[0, 0, 1], sem.at[2]),
    ]
    for copy in copies:
        copy.start()
    for copy in copies:
        copy.wait()


def shards(energies, green_free, coupling, screened, shift_offsets):
    orb = green_free.shape[-1]
    shifts = screened.shape[0]
    block = (2, orb, orb)
    hbm = pl.BlockSpec(memory_space=pltpu.HBM)
    vmem = pl.BlockSpec(memory_space=pltpu.VMEM)
    dma = pltpu.SemaphoreType.DMA
    half = jnp.bfloat16
    green, sigma = pl.pallas_call(
        functools.partial(kernel, energies),
        out_shape=(pltpu.VMEM(block, half), pltpu.VMEM(block, jnp.float32)),
        in_specs=[pl.BlockSpec(memory_space=pltpu.SMEM), hbm, hbm, hbm],
        out_specs=(vmem, vmem),
        scratch_shapes=[
            pltpu.VMEM(block, half),
            pltpu.VMEM(block, half),
            pltpu.VMEM((shifts, *block), half),
            pltpu.VMEM((3, *block), half),
            pltpu.VMEM((3, *block), half),
            *[pltpu.VMEM(block, half)] * 9,
            pltpu.VMEM((3, *block), jnp.float32),
            dma((2 + shifts,)),
            dma((10, CHUNKS)),
            dma((8, CHUNKS)),
            pltpu.SemaphoreType.REGULAR,
            pltpu.SemaphoreType.REGULAR,
        ],
        compiler_params=pltpu.CompilerParams(
            collective_id=0, has_side_effects=True, vmem_limit_bytes=57 * 2**20
        ),
    )(shift_offsets, green_free, coupling, screened)
    return pl.pallas_call(
        store,
        out_shape=(
            jax.ShapeDtypeStruct(green_free.shape, half),
            jax.ShapeDtypeStruct(green_free.shape, jnp.float32),
        ),
        in_specs=[vmem, vmem],
        out_specs=(hbm, hbm),
        scratch_shapes=[dma((3,))],
        compiler_params=pltpu.CompilerParams(vmem_limit_bytes=8 * 2**20),
    )(green, sigma)


def solution(mesh):
    placed = (
        P("energy", "slab", None, None, None),
        P("slab", None, None, None),
        P(None, "slab", None, None, None),
        P(),
    )
    return jax.shard_map(
        functools.partial(shards, mesh.shape["energy"]),
        mesh=mesh,
        in_specs=placed,
        out_specs=(P("energy", "slab", None, None, None), P("energy", "slab", None, None, None)),
        check_vma=False,
    )
```

```python
import functools

import jax
import jax.numpy as jnp
from jax import lax
from jax.experimental import pallas as pl
from jax.experimental.pallas import tpu as pltpu
from jax.sharding import PartitionSpec as P

MESH = pl.DeviceIdType.MESH
CHUNKS = 2
STEPS = 2
CHAIN, CROSS, BEYOND, NEAR, FAR, FREE_NEAR, FREE_FAR, SEAM, WRAP, WRAP_TWO = range(10)
OWN, BESIDE, REMOTE = range(3)


def dot(a, b):
    return jnp.dot(a, b, preferred_element_type=jnp.float32)


def dot_t(a, b):
    return lax.dot_general(a, b, (((0,), (0,)), ((), ())), preferred_element_type=jnp.float32)


def complex_dot(first, second_re, second_im):
    half = first.shape[0] // 2
    by_re = dot(first, second_re)
    by_im = dot(first, second_im)
    return by_re[:half] - by_im[half:], by_im[:half] + by_re[half:]


def kernel(
    energies,
    shift_ref,
    free_hbm,
    coup_hbm,
    scr_hbm,
    green,
    sig,
    free,
    coup,
    scr,
    left,
    right,
    middle,
    chain_in,
    cross_in,
    beyond_in,
    near,
    far,
    free_near,
    free_far,
    seam_in,
    weight,
    load_sem,
    send_sem,
    recv_sem,
    ready,
    near_ready,
):
    e = lax.axis_index("energy")
    s = lax.axis_index("slab")
    shifts = scr.shape[0]
    orb = free.shape[1]
    rows = orb // CHUNKS
    parity = lax.rem(e, 2)
    partner = e + 1 - 2 * parity
    onward = lax.rem(e + 2 - 4 * parity + energies, energies)
    behind = lax.rem(e - 2 + 4 * parity + energies, energies)
    landing = (chain_in, cross_in, beyond_in, near, far, free_near, free_far, seam_in)

    load_free = pltpu.make_async_copy(free_hbm.at[0, 0], free, load_sem.at[0])
    load_coup = pltpu.make_async_copy(coup_hbm.at[0], coup, load_sem.at[1])
    loads = [
        pltpu.make_async_copy(scr_hbm.at[k, 0], scr.at[k], load_sem.at[2 + k])
        for k in range(shifts)
    ]
    barrier = pltpu.get_barrier_semaphore()

    def greet(device):
        pl.semaphore_signal(barrier, inc=1, device_id=device, device_id_type=MESH)

    last = energies - 1
    is_first = e == 0
    is_last = e == last
    has_onward = e != last - 1
    far_side = jnp.where(s == 2, 3, s)

    lead = jnp.logical_and(is_last, s == 0)

    @pl.when(jnp.logical_or(s > 0, jnp.logical_and(e > 0, has_onward)))
    def _():
        greet((partner, s))

    @pl.when(s == 1)
    def _():
        greet((e, 0))

    @pl.when(s == 2)
    def _():
        greet((partner, 1))
        greet((e, 3))

    @pl.when(s == 3)
    def _():
        greet((e, 2))

    @pl.when(jnp.logical_or(onward > e, lead))
    def _():
        greet((onward, far_side))

    led = jnp.logical_and(e == last - 2, s == 0)
    greets_behind = jnp.logical_and(behind > e, jnp.logical_not(led))

    @pl.when(jnp.logical_and(e > 0, jnp.logical_and(greets_behind, s != 2)))
    def _():
        greet((behind, s))

    @pl.when(jnp.logical_and(e > 0, jnp.logical_and(behind > e, s == 3)))
    def _():
        greet((behind, 2))

    @pl.when(jnp.logical_and(is_first, s < 3))
    def _():
        greet((last, jnp.where(s == 2, 2, 0)))

    @pl.when(jnp.logical_and(is_last, s == 0))
    def _():
        greet((last, 1))

    @pl.when(jnp.logical_and(is_first, s == 2))
    def _():
        greet((last, 1))

    load_free.start()
    load_coup.start()

    def meet(row, senders, wrapped):
        waits = jnp.logical_and(has_onward, jnp.logical_and(onward < e, jnp.logical_not(lead)))
        answers = jnp.logical_or(behind < e, led)
        below = jnp.where(waits, 1, 0) + jnp.where(is_last, wrapped, 0)
        below = below + jnp.where(answers, senders, 0)
        pl.semaphore_wait(barrier, row + below)
        if senders:

            @pl.when(answers)
            def _():
                for sender in range(senders):
                    pl.semaphore_signal(
                        ready, inc=1, device_id=(behind, s - sender), device_id_type=MESH
                    )

    def meet_onward():
        @pl.when(jnp.logical_or(onward > e, lead))
        def _():
            pl.semaphore_wait(ready, 1)

    def load_screened():
        for load in loads:
            load.start()

    def move(kind, source, device, c, sender=None):
        sender = kind if sender is None else sender
        part = pl.ds(c * rows, rows)
        return pltpu.make_async_remote_copy(
            src_ref=source.at[:, part],
            dst_ref=landing[kind].at[:, part],
            send_sem=send_sem.at[sender, c],
            recv_sem=recv_sem.at[kind, c],
            device_id=device,
            device_id_type=MESH,
        )

    def arrived(kind, c):
        move(kind, free, (partner, s), c).wait_recv()

    def all_arrived(kind):
        for c in range(CHUNKS):
            arrived(kind, c)

    def sent(kind):
        for c in range(CHUNKS):
            move(0, free, (partner, s), c, kind).wait_send()

    def maps(block, slot):
        re, im = complex_dot(block[...].reshape(2 * orb, orb), coup[0], coup[1])
        left[slot, 0] = re.astype(jnp.bfloat16)
        left[slot, 1] = im.astype(jnp.bfloat16)
        re = dot_t(coup[0], block[0]) + dot_t(coup[1], block[1])
        im = dot_t(coup[0], block[1]) - dot_t(coup[1], block[0])
        right[slot, 0] = re.astype(jnp.bfloat16)
        right[slot, 1] = im.astype(jnp.bfloat16)

    def advance(slot, before, block, result, done=None):
        re, im = complex_dot(left[slot].reshape(2 * orb, orb), before[0], before[1])
        middle[0] = re.astype(jnp.bfloat16)
        middle[1] = im.astype(jnp.bfloat16)
        high = orb // STEPS
        for step in range(STEPS):
            part = pl.ds(step * high, high)
            stacked = middle[:, part, :].reshape(2 * high, orb)
            re, im = complex_dot(stacked, right[slot, 0], right[slot, 1])
            result[0, part, :] = (block[0, part, :].astype(jnp.float32) + re).astype(jnp.bfloat16)
            result[1, part, :] = (block[1, part, :].astype(jnp.float32) + im).astype(jnp.bfloat16)
            if done is not None:
                for c in range(step * CHUNKS // STEPS, (step + 1) * CHUNKS // STEPS):
                    done(c)

    def sum_weights():
        for load in loads:
            load.wait()
        near_shift = 2 * parity - 1

        @pl.loop(0, orb // 16)
        def _(step):
            part = pl.ds(pl.multiple_of(step * 16, 16), 16)
            total = [jnp.zeros((2, 16, orb), jnp.float32) for _ in range(3)]
            for k in range(shifts):
                block = scr[k, :, part, :].astype(jnp.float32)
                for slot, value in enumerate((0, near_shift, -near_shift)):
                    total[slot] = total[slot] + jnp.where(shift_ref[k] == value, block, 0.0)
            for slot in range(3):
                weight[slot, :, part, :] = total[slot]

    def term(block, slot, part):
        re = block[0, part, :].astype(jnp.float32)
        im = block[1, part, :].astype(jnp.float32)
        weight_re = weight[slot, 0, part, :]
        weight_im = weight[slot, 1, part, :]
        return re * weight_re - im * weight_im, re * weight_im + im * weight_re

    def begin_sigma(c):
        part = pl.ds(c * rows, rows)
        own = term(green, OWN, part)
        beside = term(near, BESIDE, part)
        sig[0, part, :] = -(own[1] + beside[1])
        sig[1, part, :] = own[0] + beside[0]

    def end_sigma(c):
        part = pl.ds(c * rows, rows)
        remote = term(far, REMOTE, part)
        sig[0, part, :] = sig[0, part, :] - remote[1]
        sig[1, part, :] = sig[1, part, :] + remote[0]

    @pl.when(s == 0)
    def _():
        meet(jnp.where(jnp.logical_or(e == 1, is_last), 1, 2), 1, 2)
        for c in range(CHUNKS):
            move(CHAIN, free_hbm.at[0, 0], (e, 1), c).start()
        load_free.wait()

        @pl.when(is_last)
        def _():
            for c in range(CHUNKS):
                move(FAR, free, (0, s), c, WRAP).start()
            for c in range(CHUNKS):
                arrived(SEAM, c)
                move(FAR, seam_in, (0, 1), c, WRAP_TWO).start()

        @pl.when(jnp.logical_or(is_first, e == last - 1))
        def _():
            pl.semaphore_signal(near_ready, inc=1, device_id=(partner, 0), device_id_type=MESH)

        @pl.when(e == 1)
        def _():
            pl.semaphore_wait(near_ready, 1)

        @pl.when(jnp.logical_not(is_last))
        def _():
            for c in range(CHUNKS):
                move(NEAR, free, (partner, s), c).start()

        load_screened()
        green[...] = free[...]
        sum_weights()
        meet_onward()
        for c in range(CHUNKS):
            arrived(NEAR, c)

            @pl.when(has_onward)
            def _():
                move(FAR, near, (onward, s), c).start()

            begin_sigma(c)

        @pl.when(is_last)
        def _():
            pl.semaphore_wait(near_ready, 1)
            for c in range(CHUNKS):
                move(NEAR, free, (partner, s), c).start()

        for c in range(CHUNKS):
            arrived(FAR, c)
            end_sigma(c)
        load_coup.wait()
        sent(CHAIN)
        sent(NEAR)

        @pl.when(is_last)
        def _():
            sent(WRAP)
            sent(WRAP_TWO)

        @pl.when(has_onward)
        def _():
            sent(FAR)

    @pl.when(s == 1)
    def _():
        def relay(c):
            arrived(NEAR, c)
            move(CHAIN, near, (partner, 2), c).start()

        load_free.wait()
        load_coup.wait()
        maps(free, OWN)
        meet(2, 1, 2)

        @pl.when(is_first)
        def _():
            for c in range(CHUNKS):
                relay(c)

        all_arrived(CHAIN)

        def hand_on(c):
            @pl.when(is_last)
            def _():
                move(BEYOND, green, (0, 2), c, WRAP).start()

            @pl.when(jnp.logical_not(is_last))
            def _():
                move(CROSS, green, (partner, 2), c).start()

        advance(OWN, chain_in, free, green, hand_on)

        @pl.when(is_last)
        def _():
            for c in range(CHUNKS):
                move(SEAM, green, (e, 0), c).start()
            sent(WRAP)
            for c in range(CHUNKS):
                move(CROSS, green, (partner, 2), c).start()
            sent(SEAM)

        for c in range(CHUNKS):
            move(NEAR, green, (partner, s), c).start()
        load_screened()
        sum_weights()

        @pl.when(e > 0)
        def _():
            for c in range(CHUNKS):
                relay(c)

        meet_onward()
        for c in range(CHUNKS):

            @pl.when(has_onward)
            def _():
                move(FAR, near, (onward, s), c).start()

            begin_sigma(c)
        for c in range(CHUNKS):
            arrived(FAR, c)
            end_sigma(c)
        sent(CROSS)
        sent(NEAR)
        sent(CHAIN)

        @pl.when(has_onward)
        def _():
            sent(FAR)

    @pl.when(s == 2)
    def _():
        load_free.wait()
        meet(2, 0, 1)

        @pl.when(is_last)
        def _():
            for c in range(CHUNKS):
                move(FREE_FAR, free, (0, 2), c, WRAP).start()
            sent(WRAP)

        for c in range(CHUNKS):
            move(FREE_NEAR, free, (partner, s), c).start()
        load_coup.wait()
        load_screened()
        maps(free, OWN)
        sum_weights()
        all_arrived(FREE_NEAR)
        maps(free_near, BESIDE)
        all_arrived(CROSS)
        advance(BESIDE, cross_in, free_near, near, lambda c: move(CROSS, near, (e, 3), c).start())
        meet_onward()

        @pl.when(has_onward)
        def _():
            for c in range(CHUNKS):
                move(BEYOND, near, (onward, 3), c).start()

        all_arrived(CHAIN)
        advance(OWN, chain_in, free, green, lambda c: move(CHAIN, green, (e, 3), c).start())
        for c in range(CHUNKS):
            begin_sigma(c)

        @pl.when(is_first)
        def _():
            all_arrived(FREE_FAR)
            maps(free_far, REMOTE)
            all_arrived(BEYOND)
            advance(
                REMOTE,
                beyond_in,
                free_far,
                far,
                lambda c: move(BEYOND, far, (e, 3), c, WRAP).start(),
            )

        @pl.when(e > 0)
        def _():
            all_arrived(FAR)

        for c in range(CHUNKS):
            end_sigma(c)
        sent(FREE_NEAR)
        sent(CROSS)
        sent(CHAIN)

        @pl.when(has_onward)
        def _():
            sent(BEYOND)

        @pl.when(is_first)
        def _():
            sent(WRAP)

    @pl.when(s == 3)
    def _():
        load_free.wait()
        load_coup.wait()
        load_screened()
        meet(2, 2, 0)

        @pl.when(is_last)
        def _():
            for c in range(CHUNKS):
                move(SEAM, free, (1, 3), c).start()

        maps(free, OWN)
        sum_weights()

        @pl.when(is_last)
        def _():
            sent(SEAM)

        for c in range(CHUNKS):
            move(FREE_NEAR, free, (partner, s), c).start()
        meet_onward()
        for c in range(CHUNKS):
            arrived(FREE_NEAR, c)

            @pl.when(has_onward)
            def _():
                move(FREE_FAR, free_near, (onward, s), c).start()

        maps(free_near, BESIDE)
        all_arrived(CROSS)
        advance(BESIDE, cross_in, free_near, near)

        @pl.when(e > 0)
        def _():
            all_arrived(FREE_FAR)
            maps(free_far, REMOTE)

        all_arrived(CHAIN)
        advance(OWN, chain_in, free, green)

        @pl.when(e == 1)
        def _():
            for c in range(CHUNKS):
                arrived(SEAM, c)
                move(FREE_FAR, seam_in, (0, 3), c, WRAP).start()

        for c in range(CHUNKS):
            begin_sigma(c)

        @pl.when(is_first)
        def _():
            all_arrived(FREE_FAR)
            maps(free_far, REMOTE)

        for c in range(CHUNKS):
            arrived(BEYOND, c)

            @pl.when(e > 0)
            def _():
                move(FAR, beyond_in, (e, 2), c).start()

        advance(REMOTE, beyond_in, free_far, far, end_sigma)
        sent(FREE_NEAR)

        @pl.when(e == 1)
        def _():
            sent(WRAP)

        @pl.when(has_onward)
        def _():
            sent(FREE_FAR)

        @pl.when(e > 0)
        def _():
            sent(FAR)


def store(green, sig, green_hbm, sigma_hbm, sem):
    copies = [
        pltpu.make_async_copy(green, green_hbm.at[0, 0], sem.at[0]),
        pltpu.make_async_copy(sig.at[0], sigma_hbm.at[0, 0, 0], sem.at[1]),
        pltpu.make_async_copy(sig.at[1], sigma_hbm.at[0, 0, 1], sem.at[2]),
    ]
    for copy in copies:
        copy.start()
    for copy in copies:
        copy.wait()


def shards(energies, green_free, coupling, screened, shift_offsets):
    orb = green_free.shape[-1]
    shifts = screened.shape[0]
    block = (2, orb, orb)
    hbm = pl.BlockSpec(memory_space=pltpu.HBM)
    vmem = pl.BlockSpec(memory_space=pltpu.VMEM)
    dma = pltpu.SemaphoreType.DMA
    half = jnp.bfloat16
    green, sigma = pl.pallas_call(
        functools.partial(kernel, energies),
        out_shape=(pltpu.VMEM(block, half), pltpu.VMEM(block, jnp.float32)),
        in_specs=[pl.BlockSpec(memory_space=pltpu.SMEM), hbm, hbm, hbm],
        out_specs=(vmem, vmem),
        scratch_shapes=[
            pltpu.VMEM(block, half),
            pltpu.VMEM(block, half),
            pltpu.VMEM((shifts, *block), half),
            pltpu.VMEM((3, *block), half),
            pltpu.VMEM((3, *block), half),
            *[pltpu.VMEM(block, half)] * 9,
            pltpu.VMEM((3, *block), jnp.float32),
            dma((2 + shifts,)),
            dma((10, CHUNKS)),
            dma((8, CHUNKS)),
            pltpu.SemaphoreType.REGULAR,
            pltpu.SemaphoreType.REGULAR,
        ],
        compiler_params=pltpu.CompilerParams(
            collective_id=0, has_side_effects=True, vmem_limit_bytes=57 * 2**20
        ),
    )(shift_offsets, green_free, coupling, screened)
    return pl.pallas_call(
        store,
        out_shape=(
            jax.ShapeDtypeStruct(green_free.shape, half),
            jax.ShapeDtypeStruct(green_free.shape, jnp.float32),
        ),
        in_specs=[vmem, vmem],
        out_specs=(hbm, hbm),
        scratch_shapes=[dma((3,))],
        compiler_params=pltpu.CompilerParams(vmem_limit_bytes=8 * 2**20),
    )(green, sigma)


def solution(mesh):
    placed = (
        P("energy", "slab", None, None, None),
        P("slab", None, None, None),
        P(None, "slab", None, None, None),
        P(),
    )
    return jax.shard_map(
        functools.partial(shards, mesh.shape["energy"]),
        mesh=mesh,
        in_specs=placed,
        out_specs=(P("energy", "slab", None, None, None), P("energy", "slab", None, None, None)),
        check_vma=False,
    )
```
